256 devices in a mesh: sub: 64 (over y, z, core), grp: 4 (over x).
Axes of the slice: x: 4, y: 4, z: 8, core: 2. Of those that a mesh axis runs over, the one named last changes fastest.
Arguments:
- interface_values: float32 [4, 64, 16, 128], P('grp', 'sub'), may hold values from 0.1 to 10
- send_blocks: int32 [4, 64, 4, 8], P('grp', 'sub'), may hold values from 0 to 15
- recv_blocks: int32 [4, 64, 4, 8], P('grp', 'sub'), may hold values from 0 to 15
- block_counts: int32 [4, 64, 4], P('grp', 'sub'), may hold values from 1 to 8, as said below
- live_sizes: int32 [4, 64], P('grp', 'sub'), may hold values from 1 to 2048, 43690 in all within a row
- schur: bfloat16 [4, 64, 2048, 2048], P('grp', 'sub'), may hold values from -0.125 to 0.125
- basis: bfloat16 [4, 64, 96, 2048], P('grp', 'sub'), may hold values from -6 to 6
- coarse_map: int32 [4, 64, 96], P('grp'), may hold values from 0 to 1023, as said below
Outputs:
- weights: float32 [4, 64, 16, 128], P('grp', 'sub')
- schur_image: bfloat16 [4, 64, 96, 2048], P('grp', 'sub')
- coarse: float32 [4, 1024, 1024], P('grp', 'sub')
The draws below stay inside these ranges and needn't reach their ends.
Inputs may be any that keep to these rules, and one draw needn't show every extreme that they name: `block_counts`: toward direction 0 some subdomain of each group fills all 8 slots. `live_sizes`: within one group the live sizes sum to 43690, and the largest is 2048. `coarse_map`: the 96 coarse unknowns of one subdomain are distinct.
All inputs are finite; a program needn't handle non-finite values.
Results may differ from the reference program's by a relative error of at most 0.0042.
Values may be sent and summed in bfloat16 or wider, within the bound.
A program may use at most 64 MiB of HBM per device.

```python
import math
import jax
import jax.numpy as jnp
import numpy as np
from jax import lax

NI = 2048
BR = 128
NB = 16
NP = 96
FB = 8
NCS = 1024
N_SUB = 64
N_GRP = 4


def draw_block_counts(key, part):
    key = jax.random.fold_in(key, 3)
    base_key, hot_key = jax.random.split(key)
    counts = jax.random.randint(base_key, (N_GRP, N_SUB, 4), 1, FB + 1)
    full_row = jax.random.randint(hot_key, (N_GRP, 1, 1), 0, N_SUB)
    full_slot = (jnp.arange(N_SUB)[None, :, None] == full_row) & (jnp.arange(4)[None, None, :] == 0)
    return jnp.where(full_slot, FB, counts).astype(jnp.int32)


def drawn_picks(one_key):
    return jax.random.permutation(one_key, NCS)[:NP].astype(jnp.int32)


def covering_picks(one_key):
    inner_key, order_key = jax.random.split(one_key)
    inner_values = (jax.random.permutation(inner_key, NCS - 2)[:NP - 2] + 1).astype(jnp.int32)
    corner_values = jnp.array([0, NCS - 1], jnp.int32)
    joined = jnp.concatenate([inner_values, corner_values])
    return joined[jax.random.permutation(order_key, NP)]


def draw_coarse_map(key, part):
    key = jax.random.fold_in(key, 5)
    pick_key, cover_key, row_key = jax.random.split(key, 3)
    drawn = jax.vmap(drawn_picks)(jax.random.split(pick_key, N_GRP * N_SUB)).reshape(N_GRP, N_SUB, NP)
    covering = jax.vmap(covering_picks)(jax.random.split(cover_key, N_GRP)).reshape(N_GRP, 1, NP)
    chosen_row = jax.random.randint(row_key, (N_GRP, 1, 1), 0, N_SUB)
    return jnp.where(jnp.arange(N_SUB)[None, :, None] == chosen_row, covering, drawn).astype(jnp.int32)


def touch_ends(values, stream_key, least, top_value):
    extent = values.shape
    index_at = [jax.random.randint(jax.random.fold_in(stream_key, axis), (), 0, extent[axis]) for axis in range(len(extent))]
    values = values.at[tuple(index_at)].set(least)
    longest = extent.index(max(extent))
    index_at[longest] = (index_at[longest] + 1) % extent[longest]
    return values.at[tuple(index_at)].set(top_value)


def level_of(own_key, dims, cuts, least, top_value):
    gain = 1.0
    for axis_at, shards_of in cuts:
        steps = jax.random.uniform(jax.random.fold_in(jax.random.fold_in(own_key, 6), axis_at), (shards_of,), jnp.float32, least / len(cuts), top_value / len(cuts))
        gain = gain * jnp.repeat(jnp.exp(steps), dims[axis_at] // shards_of).reshape((-1,) + (1,) * (len(dims) - 1 - axis_at))
    return gain


def length_profile(amount, total, reach, slope):
    portions = [(1 << 20) // math.isqrt(standing ** slope) + 1 for standing in range(2, amount + 1)]
    rest, given = total - reach - (amount - 1), [1] * (amount - 1)
    while rest > 0:
        movable = [i for i in range(amount - 1) if given[i] < reach]
        pool, left = sum([portions[i] for i in movable]), rest
        for i in movable:
            extra = min(reach - given[i], max(1, left * portions[i] // pool), rest)
            given[i] = given[i] + extra
            rest = rest - extra
    return np.array([reach] + given)


def ragged(key, count, total, most, lean):
    if count == 2:
        one = jax.random.randint(key, (), max(1, total - most), min(most, total - 1) + 1)
        return jnp.stack([one, total - one])
    sizes = jnp.asarray(length_profile(count, total, most, lean), jnp.int32)
    twos = (count - 1) // 2
    donor, taker = sizes[1:1 + 2 * twos:2], sizes[2:2 + 2 * twos:2]
    room = jnp.minimum(donor - 1, most - taker)
    passed = jax.random.randint(jax.random.fold_in(key, 1), (twos,), 0, 1 << 20) % (room + 1)
    sizes = sizes.at[1:1 + 2 * twos:2].set(donor - passed).at[2:2 + 2 * twos:2].set(taker + passed)
    return sizes[jax.random.permutation(jax.random.fold_in(key, 2), count)]


def noise(stream_key, shape, spread, most, pieces=(), dtype=jnp.bfloat16):
    drawn = spread * jax.random.normal(stream_key, shape, jnp.float32)
    if pieces:
        drawn = drawn * level_of(stream_key, shape, pieces, -0.22, 0.18)
    return jnp.clip(drawn, -most, most).astype(dtype)


def setup_inputs(seed: int = 0) -> dict:
    arg_keys = jax.random.split(jax.random.key(seed), 9)
    return {
        "interface_values": jnp.clip(jnp.exp(math.log(10.0) - 4.6051702 * jax.random.uniform(arg_keys[0], (N_GRP, N_SUB, NB, BR), jnp.float32) ** level_of(arg_keys[0], (N_GRP, N_SUB, NB, BR), ((0, 4), (1, 64)), -0.2, 0.2)), 0.1, 10.0),
        "send_blocks": touch_ends(jax.random.randint(arg_keys[1], (N_GRP, N_SUB, 4, FB), 0, NB), jax.random.fold_in(arg_keys[1], 1), 0, NB - 1).astype(jnp.int32),
        "recv_blocks": touch_ends(jax.random.randint(arg_keys[2], (N_GRP, N_SUB, 4, FB), 0, NB), jax.random.fold_in(arg_keys[2], 1), 0, NB - 1).astype(jnp.int32),
        "block_counts": draw_block_counts(jax.random.fold_in(arg_keys[8], 71), 0),
        "live_sizes": jax.vmap(lambda own: ragged(own, N_SUB, N_SUB * NI // 3, NI, 2))(jax.random.split(arg_keys[4], N_GRP)).reshape((N_GRP, N_SUB)).astype(jnp.int32),
        "schur": noise(arg_keys[5], (N_GRP, N_SUB, NI, NI), NI ** -0.5, 0.125, ((0, 4), (1, 64))),
        "basis": noise(arg_keys[6], (N_GRP, N_SUB, NP, NI), 1.0, 6.0, ((0, 4), (1, 64))),
        "coarse_map": draw_coarse_map(jax.random.fold_in(arg_keys[8], 71), 0),
    }


def subdomain_image(inputs):
    matrix, primal_basis, weight_rows, live_size = inputs
    live_mask = (jnp.arange(NI) < live_size).astype(jnp.float32)
    scaled = (primal_basis.astype(jnp.float32) * (weight_rows.reshape(NI) * live_mask)[None, :]).astype(jnp.bfloat16)
    images = lax.dot_general(scaled, matrix, (((1,), (1,)), ((), ())), preferred_element_type=jnp.float32)
    images = images * live_mask[None, :]
    partial_value = lax.dot_general(scaled.astype(jnp.float32), images, (((1,), (1,)), ((), ())), precision=lax.Precision.HIGHEST) / NI
    return images.astype(jnp.bfloat16), partial_value.astype(jnp.bfloat16)


def reference(interface_values, send_blocks, recv_blocks, block_counts, live_sizes, schur, basis, coarse_map):
    blocks = jnp.arange(NB)
    chosen = (send_blocks[..., None] == blocks).astype(jnp.float32)
    filled = (jnp.arange(FB)[None, None, None, :] < block_counts[..., None]).astype(jnp.float32)
    packed = jnp.einsum('gsjfn,gsnb->gsjfb', chosen, interface_values, precision=lax.Precision.HIGHEST) * filled[..., None]
    from_lower = jnp.roll(packed[:, :, 0], 1, axis=1)
    from_upper = jnp.roll(packed[:, :, 1], -1, axis=1)
    nothing = jnp.zeros_like(packed[:1, :, 2])
    from_below = jnp.concatenate([nothing, packed[:-1, :, 2]], axis=0)
    from_above = jnp.concatenate([packed[1:, :, 3], nothing], axis=0)
    arrived = jnp.stack([from_lower, from_upper, from_below, from_above], axis=2)
    placed = (recv_blocks[..., None] == blocks).astype(jnp.float32)
    totals = interface_values + jnp.einsum('gsjfn,gsjfb->gsnb', placed, arrived, precision=lax.Precision.HIGHEST)
    weights = interface_values / totals
    count_all = N_GRP * N_SUB
    images, partials = lax.map(subdomain_image, (schur.reshape(count_all, NI, NI), basis.reshape(count_all, NP, NI), weights.reshape(count_all, NB, BR), live_sizes.reshape(count_all)))
    schur_image = images.reshape(N_GRP, N_SUB, NP, NI)
    partials = partials.reshape(N_GRP, N_SUB, NP, NP).astype(jnp.float32)
    sections = []
    for group in range(N_GRP):
        owner_map = coarse_map[group]
        section = jnp.zeros((NCS, NCS), jnp.float32)
        section = section.at[owner_map[:, :, None], owner_map[:, None, :]].add(partials[group])
        sections.append(section)
    coarse = jnp.stack(sections)
    return weights, schur_image, coarse
```

```python
import functools

import jax
import jax.numpy as jnp
from jax import lax
from jax.experimental import pallas as pl
from jax.experimental.pallas import tpu as pltpu
from jax.sharding import PartitionSpec as P

MESH = pl.DeviceIdType.MESH
LANES = 128
TILE = 256


def nt(left, right):
    return lax.dot_general(
        left, right, (((1,), (1,)), ((), ())), preferred_element_type=jnp.float32
    )


def nn(left, right):
    return lax.dot_general(
        left, right, (((1,), (0,)), ((), ())), preferred_element_type=jnp.float32
    )


def kernel(
    n_sub,
    n_grp,
    send_s,
    recv_s,
    counts_s,
    live_s,
    values_h,
    schur_h,
    basis_h,
    map_h,
    weights_h,
    image_h,
    coarse_h,
    values,
    basis,
    schur,
    cmap,
    packed,
    arrived,
    weights,
    scaled,
    image,
    part,
    row_pick,
    outgoing,
    incoming,
    high_pick,
    low_pick,
    spread,
    coarse,
    load_sem,
    schur_sem,
    store_sem,
    near_send,
    near_recv,
    far_send,
    far_recv,
):
    me = lax.axis_index("sub")
    group = lax.axis_index("grp")
    interface = schur.shape[0]
    columns = basis.shape[0]
    blocks = values.shape[0]
    rows = incoming.shape[1]
    section = rows * n_sub
    highs = section // LANES

    loads = [
        pltpu.make_async_copy(values_h.at[0, 0], values, load_sem.at[0]),
        pltpu.make_async_copy(map_h.at[0], cmap, load_sem.at[1]),
        pltpu.make_async_copy(basis_h.at[0, 0], basis, load_sem.at[2]),
    ]
    for load in loads:
        load.start()

    barrier = pltpu.get_barrier_semaphore()
    up = lax.rem(group + 1, n_grp)
    down = lax.rem(group + n_grp - 1, n_grp)
    pl.semaphore_signal(barrier, inc=1, device_id={"grp": up}, device_id_type=MESH)
    pl.semaphore_signal(barrier, inc=1, device_id={"grp": down}, device_id_type=MESH)

    def greet(step, carry):
        peer = lax.rem(me + step, n_sub)
        pl.semaphore_signal(barrier, inc=1, device_id={"sub": peer}, device_id_type=MESH)
        return carry

    lax.fori_loop(1, n_sub, greet, 0)

    tiles = interface // TILE
    schur_loads = [
        pltpu.make_async_copy(
            schur_h.at[0, 0, pl.ds(t * TILE, TILE)],
            schur.at[pl.ds(t * TILE, TILE)],
            schur_sem.at[t],
        )
        for t in range(tiles)
    ]
    for load in schur_loads:
        load.start()

    loads[0].wait()
    slots = packed.shape[1]
    for j in range(4):
        for f in range(slots):
            row = values[pl.ds(send_s[0, 0, j, f], 1), :]
            packed[j, f : f + 1, :] = jnp.where(f < counts_s[0, 0, j], row, 0.0)

    pl.semaphore_wait(barrier, n_sub + 1)

    right = lax.rem(me + 1, n_sub)
    left = lax.rem(me + n_sub - 1, n_sub)
    targets = [{"sub": right}, {"sub": left}, {"grp": up}, {"grp": down}]
    near = [
        pltpu.make_async_remote_copy(
            src_ref=packed.at[j],
            dst_ref=arrived.at[j],
            send_sem=near_send.at[j],
            recv_sem=near_recv.at[j],
            device_id=targets[j],
            device_id_type=MESH,
        )
        for j in range(4)
    ]
    for copy in near:
        copy.start()

    loads[1].wait()
    mine = cmap[pl.ds(me, 1), :]
    row_at = lax.broadcasted_iota(jnp.int32, (section, columns), 0)
    row_pick[...] = jnp.where(row_at == mine, 1.0, 0.0).astype(jnp.bfloat16)

    pad = jnp.full((1, LANES - columns), -1, jnp.int32)
    high_at = lax.broadcasted_iota(jnp.int32, (highs * rows, LANES), 0) // rows
    low_at = lax.broadcasted_iota(jnp.int32, (LANES, LANES), 0)

    def low(i, carry):
        row = jnp.concatenate([cmap[pl.ds(i, 1), :], pad], axis=1)
        at = pl.ds(pl.multiple_of(i * LANES, LANES), LANES)
        low_pick[:, at] = jnp.where(low_at == (row & (LANES - 1)), 1.0, 0.0).astype(jnp.bfloat16)
        return carry

    lax.fori_loop(0, n_sub, low, 0)
    part[...] = jnp.zeros_like(part)

    for copy in near:
        copy.wait()
    own = values[...]
    totals = own
    block_at = lax.broadcasted_iota(jnp.int32, own.shape, 0)
    for j in range(4):
        came = arrived[j]
        if j == 2:
            came = jnp.where(group > 0, came, 0.0)
        if j == 3:
            came = jnp.where(group < n_grp - 1, came, 0.0)
        for f in range(slots):
            totals += jnp.where(block_at == recv_s[0, 0, j, f], came[f : f + 1, :], 0.0)
    weight = own / totals
    weights[...] = weight
    weights_out = pltpu.make_async_copy(weights, weights_h.at[0, 0], store_sem.at[0])
    weights_out.start()

    live_size = live_s[0, 0]
    unknown = block_at * LANES + lax.broadcasted_iota(jnp.int32, own.shape, 1)
    live_weight = jnp.where(unknown < live_size, weight, 0.0)
    loads[2].wait()
    for n in range(blocks):
        at = slice(n * LANES, (n + 1) * LANES)
        scaled[:, at] = (basis[:, at].astype(jnp.float32) * live_weight[n : n + 1, :]).astype(
            jnp.bfloat16
        )

    total = jnp.zeros((columns, columns), jnp.float32)
    for t in range(tiles):
        at = slice(t * TILE, (t + 1) * TILE)
        schur_loads[t].wait()
        value = nt(scaled[...], schur[at, :])
        column = t * TILE + lax.broadcasted_iota(jnp.int32, value.shape, 1)
        value = jnp.where(column < live_size, value, 0.0)
        top = value.astype(jnp.bfloat16)
        rest = (value - top.astype(jnp.float32)).astype(jnp.bfloat16)
        image[:, at] = top
        total += nt(scaled[:, at], top) + nt(scaled[:, at], rest)
    image_out = pltpu.make_async_copy(image, image_h.at[0, 0], store_sem.at[1])
    image_out.start()
    part[:columns, :columns] = (total / interface).astype(jnp.bfloat16)

    picked = nn(row_pick[...], part[:columns, :])
    outgoing[...] = picked.astype(jnp.bfloat16).reshape(outgoing.shape)

    def far(step):
        peer = lax.rem(me + step, n_sub)
        return pltpu.make_async_remote_copy(
            src_ref=outgoing.at[peer],
            dst_ref=incoming.at[me],
            send_sem=far_send.at[step],
            recv_sem=far_recv.at[me],
            device_id={"sub": peer},
            device_id_type=MESH,
        )

    def send(step, carry):
        far(step).start()
        return carry

    lax.fori_loop(1, n_sub, send, 0)

    def high(i, carry):
        row = jnp.concatenate([cmap[pl.ds(i, 1), :], pad], axis=1)
        at = pl.ds(pl.multiple_of(i * LANES, LANES), LANES)
        high_pick[:, at] = jnp.where(high_at == (row >> 7), 1.0, 0.0).astype(jnp.bfloat16)
        return carry

    lax.fori_loop(0, n_sub, high, 0)

    def arrive(step, carry):
        source = lax.rem(me + step, n_sub)
        pltpu.make_async_copy(
            incoming.at[source], incoming.at[source], far_recv.at[source]
        ).wait()
        return carry

    lax.fori_loop(1, n_sub, arrive, 0)
    incoming[pl.ds(me, 1)] = outgoing[pl.ds(me, 1)]

    def fan(i, carry):
        at = pl.ds(pl.multiple_of(i * LANES, LANES), LANES)
        block = incoming[i]
        for h in range(highs):
            spread[h * rows : (h + 1) * rows, at] = (
                block * high_pick[h * rows : (h + 1) * rows, at]
            )
        return carry

    lax.fori_loop(0, n_sub, fan, 0)
    summed = nt(spread[...], low_pick[...])
    for h in range(highs):
        coarse[:, h * LANES : (h + 1) * LANES] = summed[h * rows : (h + 1) * rows, :]
    coarse_out = pltpu.make_async_copy(coarse, coarse_h.at[0], store_sem.at[2])
    coarse_out.start()

    def drain(step, carry):
        far(step).wait_send()
        return carry

    lax.fori_loop(1, n_sub, drain, 0)
    weights_out.wait()
    image_out.wait()
    coarse_out.wait()


def solution(mesh):
    n_sub, n_grp = mesh.shape["sub"], mesh.shape["grp"]

    def shards(
        interface_values, send_blocks, recv_blocks, block_counts, live_sizes, schur, basis, coarse_map
    ):
        blocks, width = interface_values.shape[2:]
        slots = send_blocks.shape[3]
        interface = schur.shape[2]
        columns = basis.shape[2]
        rows = 16
        section = rows * n_sub
        highs = section // LANES
        f32, bf16, i32 = jnp.float32, jnp.bfloat16, jnp.int32
        smem = pl.BlockSpec(memory_space=pltpu.SMEM)
        anywhere = pl.BlockSpec(memory_space=pl.ANY)
        return pl.pallas_call(
            functools.partial(kernel, n_sub, n_grp),
            out_shape=(
                jax.ShapeDtypeStruct((1, 1, blocks, width), f32),
                jax.ShapeDtypeStruct((1, 1, columns, interface), bf16),
                jax.ShapeDtypeStruct((1, rows, section), f32),
            ),
            in_specs=[smem] * 4 + [anywhere] * 4,
            out_specs=(anywhere,) * 3,
            scratch_shapes=[
                pltpu.VMEM((blocks, width), f32),
                pltpu.VMEM((columns, interface), bf16),
                pltpu.VMEM((interface, interface), bf16),
                pltpu.VMEM((n_sub, columns), i32),
                pltpu.VMEM((4, slots, width), f32),
                pltpu.VMEM((4, slots, width), f32),
                pltpu.VMEM((blocks, width), f32),
                pltpu.VMEM((columns, interface), bf16),
                pltpu.VMEM((columns, interface), bf16),
                pltpu.VMEM((LANES, LANES), bf16),
                pltpu.VMEM((section, columns), bf16),
                pltpu.VMEM((n_sub, rows, LANES), bf16),
                pltpu.VMEM((n_sub, rows, LANES), bf16),
                pltpu.VMEM((highs * rows, n_sub * LANES), bf16),
                pltpu.VMEM((LANES, n_sub * LANES), bf16),
                pltpu.VMEM((highs * rows, n_sub * LANES), bf16),
                pltpu.VMEM((rows, section), f32),
                pltpu.SemaphoreType.DMA((3,)),
                pltpu.SemaphoreType.DMA((interface // TILE,)),
                pltpu.SemaphoreType.DMA((3,)),
                pltpu.SemaphoreType.DMA((4,)),
                pltpu.SemaphoreType.DMA((4,)),
                pltpu.SemaphoreType.DMA((n_sub,)),
                pltpu.SemaphoreType.DMA((n_sub,)),
            ],
            compiler_params=pltpu.CompilerParams(
                collective_id=0, has_side_effects=True, vmem_limit_bytes=48 * 1024 * 1024
            ),
        )(
            send_blocks,
            recv_blocks,
            block_counts,
            live_sizes,
            interface_values,
            schur,
            basis,
            coarse_map,
        )

    placed = (
        P("grp", "sub", None, None),
        P("grp", "sub", None, None),
        P("grp", "sub", None, None),
        P("grp", "sub", None),
        P("grp", "sub"),
        P("grp", "sub", None, None),
        P("grp", "sub", None, None),
        P("grp", None, None),
    )
    return jax.shard_map(
        shards,
        mesh=mesh,
        in_specs=placed,
        out_specs=(P("grp", "sub", None, None), P("grp", "sub", None, None), P("grp", "sub", None)),
        check_vma=False,
    )
```

```python
import functools

import jax
import jax.numpy as jnp
from jax import lax
from jax.experimental import pallas as pl
from jax.experimental.pallas import tpu as pltpu
from jax.sharding import PartitionSpec as P

MESH = pl.DeviceIdType.MESH
LANES = 128
TILE = 256
POOL = 4


def nt(left, right):
    return lax.dot_general(
        left, right, (((1,), (1,)), ((), ())), preferred_element_type=jnp.float32
    )


def nn(left, right):
    return lax.dot_general(
        left, right, (((1,), (0,)), ((), ())), preferred_element_type=jnp.float32
    )


def exchange(
    n_sub,
    n_grp,
    live_s,
    send_h,
    recv_h,
    counts_h,
    values_h,
    schur_h,
    basis_h,
    map_h,
    weights,
    image,
    incoming,
    high_pick,
    low_pick,
    send_s,
    recv_s,
    counts_s,
    values,
    basis,
    schur,
    cmap,
    maps,
    packed,
    arrived,
    scaled,
    part,
    pool,
    terms,
    row_pick,
    outgoing,
    load_sem,
    schur_sem,
    near_send,
    near_recv,
    pool_send,
    pool_recv,
    far_send,
    far_recv,
):
    me = lax.axis_index("sub")
    group = lax.axis_index("grp")
    n_line = n_sub // POOL
    plane, place = me // n_line, lax.rem(me, n_line)
    interface = schur.shape[0]
    columns = basis.shape[0]
    blocks = values.shape[0]
    rows = incoming.shape[1]
    section = rows * n_sub
    highs = section // LANES
    slots = packed.shape[1]

    with jax.named_scope("start_loads"):
        pairs = [
            (values_h.at[0, 0], values),
            (send_h.at[0, 0], send_s),
            (counts_h.at[0], counts_s),
            (recv_h.at[0, 0], recv_s),
            (map_h.at[0], cmap),
            (basis_h.at[0, 0], basis),
        ]
        loads = [
            pltpu.make_async_copy(source, target, load_sem.at[i])
            for i, (source, target) in enumerate(pairs)
        ]
        for load in loads:
            load.start()
        tiles = interface // TILE
        schur_loads = [
            pltpu.make_async_copy(
                schur_h.at[0, 0, pl.ds(t * TILE, TILE)],
                schur.at[pl.ds(t * TILE, TILE)],
                schur_sem.at[t],
            )
            for t in range(tiles)
        ]
        for load in schur_loads:
            load.start()

    up = lax.rem(group + 1, n_grp)
    down = lax.rem(group + n_grp - 1, n_grp)
    with jax.named_scope("greet"):
        barrier = pltpu.get_barrier_semaphore()
        pl.semaphore_signal(barrier, inc=1, device_id={"grp": up}, device_id_type=MESH)
        pl.semaphore_signal(barrier, inc=1, device_id={"grp": down}, device_id_type=MESH)

        def greet(peer):
            pl.semaphore_signal(barrier, inc=1, device_id={"sub": peer}, device_id_type=MESH)

        right = lax.rem(me + 1, n_sub)
        left = lax.rem(me + n_sub - 1, n_sub)
        greet(right)
        greet(left)
        for step in range(1, POOL):
            greet(lax.rem(me + step * n_line, n_sub))
        for step in range(1, n_line):
            greet(plane * n_line + lax.rem(place + step, n_line))

    with jax.named_scope("pack"):
        for load in loads[:3]:
            load.wait()
        for j in range(4):
            for f in range(slots):
                row = values[pl.ds(send_s[j, f], 1), :]
                packed[j, f : f + 1, :] = jnp.where(f < counts_s[0, j], row, 0.0)

    with jax.named_scope("barrier"):
        pl.semaphore_wait(barrier, 4 + (POOL - 1) + (n_line - 1))

    with jax.named_scope("near_send"):
        targets = [{"sub": right}, {"sub": left}, {"grp": up}, {"grp": down}]
        near = [
            pltpu.make_async_remote_copy(
                src_ref=packed.at[j],
                dst_ref=arrived.at[j],
                send_sem=near_send.at[j],
                recv_sem=near_recv.at[j],
                device_id=targets[j],
                device_id_type=MESH,
            )
            for j in range(4)
        ]
        for copy in near:
            copy.start()

    with jax.named_scope("picks"):
        loads[4].wait()
        wide = POOL * columns
        line_map = jnp.concatenate(
            [cmap[k * n_line : (k + 1) * n_line, :] for k in range(POOL)], axis=1
        )
        maps[...] = line_map
        mine = maps[pl.ds(place, 1), :]
        own_rows = rows * n_line
        row_at = own_rows * plane + lax.broadcasted_iota(jnp.int32, (own_rows, wide), 0)
        row_pick[...] = jnp.where(row_at == mine, 1.0, 0.0).astype(jnp.bfloat16)
        low_at = lax.broadcasted_iota(jnp.int32, (LANES, wide), 0)
        high_at = lax.broadcasted_iota(jnp.int32, (highs * rows, wide), 0) // rows

        def low(i, carry):
            row = maps[pl.ds(i, 1), :]
            at = pl.ds(pl.multiple_of(i * wide, LANES), wide)
            low_pick[:, at] = jnp.where(low_at == (row & (LANES - 1)), 1.0, 0.0).astype(
                jnp.bfloat16
            )
            return carry

        lax.fori_loop(0, n_line, low, 0)
        terms[...] = jnp.zeros_like(terms)

    with jax.named_scope("near_wait"):
        for copy in near:
            copy.wait()
    with jax.named_scope("weights"):
        loads[3].wait()
        own = values[...]
        totals = own
        block_at = lax.broadcasted_iota(jnp.int32, own.shape, 0)
        for j in range(4):
            came = arrived[j]
            if j == 2:
                came = jnp.where(group > 0, came, 0.0)
            if j == 3:
                came = jnp.where(group < n_grp - 1, came, 0.0)
            for f in range(slots):
                totals += jnp.where(block_at == recv_s[j, f], came[f : f + 1, :], 0.0)
        weight = own / totals
        weights[0, 0] = weight

        live_size = live_s[0, 0]
        unknown = block_at * LANES + lax.broadcasted_iota(jnp.int32, own.shape, 1)
        live_weight = jnp.where(unknown < live_size, weight, 0.0)
    with jax.named_scope("scaled"):
        loads[5].wait()
        for n in range(blocks):
            at = slice(n * LANES, (n + 1) * LANES)
            scaled[:, at] = (basis[:, at].astype(jnp.float32) * live_weight[n : n + 1, :]).astype(
                jnp.bfloat16
            )

    with jax.named_scope("schur_wait"):
        for load in schur_loads:
            load.wait()
    with jax.named_scope("image"):
        total = jnp.zeros((columns, columns), jnp.float32)
        for t in range(tiles):
            at = slice(t * TILE, (t + 1) * TILE)
            value = nt(scaled[...], schur[at, :])
            column = t * TILE + lax.broadcasted_iota(jnp.int32, value.shape, 1)
            value = jnp.where(column < live_size, value, 0.0)
            top = value.astype(jnp.bfloat16)
            rest = (value - top.astype(jnp.float32)).astype(jnp.bfloat16)
            image[0, 0, :, at] = top
            total += nt(scaled[:, at], top) + nt(scaled[:, at], rest)
    with jax.named_scope("part"):
        value = jnp.concatenate(
            [total / interface, jnp.zeros((columns, LANES - columns), jnp.float32)], axis=1
        )
        part[...] = pltpu.roll(value, lax.rem(columns * plane, LANES), 1).astype(jnp.bfloat16)

    with jax.named_scope("pool_send"):
        shared = []
        for step in range(1, POOL):
            other = lax.rem(plane + step, POOL)
            copy = pltpu.make_async_remote_copy(
                src_ref=part,
                dst_ref=pool.at[plane],
                send_sem=pool_send.at[step],
                recv_sem=pool_recv.at[plane],
                device_id={"sub": other * n_line + place},
                device_id_type=MESH,
            )
            copy.start()
            shared.append(copy)
    with jax.named_scope("pool_wait"):
        for step in range(1, POOL):
            other = lax.rem(plane + step, POOL)
            pltpu.make_async_copy(pool.at[other], pool.at[other], pool_recv.at[other]).wait()
        pool[pl.ds(plane, 1)] = part[...][None]
    with jax.named_scope("pick_rows"):
        lane = lax.broadcasted_iota(jnp.int32, (columns, LANES), 1)
        for k in range(POOL):
            first, last = k * columns, (k + 1) * columns
            for t in range(first // LANES, (last - 1) // LANES + 1):
                inside = (lane + t * LANES >= first) & (lane + t * LANES < last)
                keep = jnp.where(inside, 1.0, 0.0).astype(jnp.bfloat16)
                terms[first:last, t * LANES : (t + 1) * LANES] = pool[k] * keep
        picked = nn(row_pick[...], terms[...])
        outgoing[...] = picked.astype(jnp.bfloat16).reshape(outgoing.shape)

    def far(step):
        peer = lax.rem(place + step, n_line)
        return pltpu.make_async_remote_copy(
            src_ref=outgoing.at[peer],
            dst_ref=incoming.at[place],
            send_sem=far_send.at[step],
            recv_sem=far_recv.at[place],
            device_id={"sub": plane * n_line + peer},
            device_id_type=MESH,
        )

    with jax.named_scope("far_send"):
        sent = [far(step) for step in range(1, n_line)]
        for copy in sent:
            copy.start()

    def high(i, carry):
        row = maps[pl.ds(i, 1), :]
        at = pl.ds(pl.multiple_of(i * wide, LANES), wide)
        high_pick[:, at] = jnp.where(high_at == (row >> 7), 1.0, 0.0).astype(jnp.bfloat16)
        return carry

    with jax.named_scope("high"):
        lax.fori_loop(0, n_line, high, 0)
    with jax.named_scope("arrive"):
        for step in range(1, n_line):
            source = lax.rem(place + n_line - step, n_line)
            pltpu.make_async_copy(
                incoming.at[source], incoming.at[source], far_recv.at[source]
            ).wait()
        incoming[pl.ds(place, 1)] = outgoing[pl.ds(place, 1)]
    with jax.named_scope("drain"):
        for copy in shared + sent:
            copy.wait_send()


def assemble(
    weights,
    image,
    incoming,
    high_pick,
    low_pick,
    weights_h,
    image_h,
    coarse_h,
    spread,
    coarse,
    store_sem,
):
    rows = incoming.shape[1]
    n_line, _, wide = incoming.shape
    highs = high_pick.shape[0] // rows
    weights_out = pltpu.make_async_copy(weights, weights_h, store_sem.at[0])
    weights_out.start()
    image_out = pltpu.make_async_copy(image, image_h, store_sem.at[1])
    image_out.start()

    def fan(i, carry):
        at = pl.ds(pl.multiple_of(i * wide, LANES), wide)
        block = incoming[i]
        for h in range(highs):
            spread[h * rows : (h + 1) * rows, at] = (
                block * high_pick[h * rows : (h + 1) * rows, at]
            )
        return carry

    with jax.named_scope("fan"):
        lax.fori_loop(0, n_line, fan, 0)
    with jax.named_scope("add"):
        summed = nt(spread[...], low_pick[...])
        for h in range(highs):
            coarse[0, :, h * LANES : (h + 1) * LANES] = summed[h * rows : (h + 1) * rows, :]
    with jax.named_scope("store"):
        coarse_out = pltpu.make_async_copy(coarse, coarse_h, store_sem.at[2])
        coarse_out.start()
        weights_out.wait()
        image_out.wait()
        coarse_out.wait()


def solution(mesh):
    n_sub, n_grp = mesh.shape["sub"], mesh.shape["grp"]

    def shards(
        interface_values, send_blocks, recv_blocks, block_counts, live_sizes, schur, basis, coarse_map
    ):
        blocks, width = interface_values.shape[2:]
        slots = send_blocks.shape[3]
        interface = schur.shape[2]
        columns = basis.shape[2]
        rows = 16
        section = rows * n_sub
        highs = section // LANES
        n_line = n_sub // POOL
        wide = POOL * columns
        f32, bf16, i32 = jnp.float32, jnp.bfloat16, jnp.int32
        hbm = pl.BlockSpec(memory_space=pltpu.HBM)
        vmem = pl.BlockSpec(memory_space=pltpu.VMEM)
        pinned = [
            pltpu.with_memory_space_constraint(x, pltpu.HBM)
            for x in (send_blocks, recv_blocks, block_counts, interface_values, schur, basis, coarse_map)
        ]
        made = pl.pallas_call(
            functools.partial(exchange, n_sub, n_grp),
            out_shape=(
                jax.ShapeDtypeStruct((1, 1, blocks, width), f32),
                jax.ShapeDtypeStruct((1, 1, columns, interface), bf16),
                jax.ShapeDtypeStruct((n_line, rows, wide), bf16),
                jax.ShapeDtypeStruct((highs * rows, n_line * wide), bf16),
                jax.ShapeDtypeStruct((LANES, n_line * wide), bf16),
            ),
            in_specs=[pl.BlockSpec(memory_space=pltpu.SMEM)] + [hbm] * 7,
            out_specs=(vmem,) * 5,
            scratch_shapes=[
                pltpu.SMEM((4, slots), i32),
                pltpu.SMEM((4, slots), i32),
                pltpu.SMEM((1, 4), i32),
                pltpu.VMEM((blocks, width), f32),
                pltpu.VMEM((columns, interface), bf16),
                pltpu.VMEM((interface, interface), bf16),
                pltpu.VMEM((n_sub, columns), i32),
                pltpu.VMEM((n_line, wide), i32),
                pltpu.VMEM((4, slots, width), f32),
                pltpu.VMEM((4, slots, width), f32),
                pltpu.VMEM((columns, interface), bf16),
                pltpu.VMEM((columns, LANES), bf16),
                pltpu.VMEM((POOL, columns, LANES), bf16),
                pltpu.VMEM((wide, wide), bf16),
                pltpu.VMEM((rows * n_line, wide), bf16),
                pltpu.VMEM((n_line, rows, wide), bf16),
                pltpu.SemaphoreType.DMA((6,)),
                pltpu.SemaphoreType.DMA((interface // TILE,)),
                pltpu.SemaphoreType.DMA((4,)),
                pltpu.SemaphoreType.DMA((4,)),
                pltpu.SemaphoreType.DMA((POOL,)),
                pltpu.SemaphoreType.DMA((POOL,)),
                pltpu.SemaphoreType.DMA((n_line,)),
                pltpu.SemaphoreType.DMA((n_line,)),
            ],
            compiler_params=pltpu.CompilerParams(
                collective_id=0, has_side_effects=True, vmem_limit_bytes=32 * 1024 * 1024
            ),
        )(live_sizes, *pinned)
        return pl.pallas_call(
            assemble,
            out_shape=(
                jax.ShapeDtypeStruct((1, 1, blocks, width), f32),
                jax.ShapeDtypeStruct((1, 1, columns, interface), bf16),
                jax.ShapeDtypeStruct((1, rows, section), f32),
            ),
            in_specs=[vmem] * 5,
            out_specs=(hbm,) * 3,
            scratch_shapes=[
                pltpu.VMEM((highs * rows, n_line * wide), bf16),
                pltpu.VMEM((1, rows, section), f32),
                pltpu.SemaphoreType.DMA((3,)),
            ],
            compiler_params=pltpu.CompilerParams(vmem_limit_bytes=16 * 1024 * 1024),
        )(*made)

    placed = (
        P("grp", "sub", None, None),
        P("grp", "sub", None, None),
        P("grp", "sub", None, None),
        P("grp", "sub", None),
        P("grp", "sub"),
        P("grp", "sub", None, None),
        P("grp", "sub", None, None),
        P("grp", None, None),
    )
    return jax.shard_map(
        shards,
        mesh=mesh,
        in_specs=placed,
        out_specs=(P("grp", "sub", None, None), P("grp", "sub", None, None), P("grp", "sub", None)),
        check_vma=False,
    )
```

```python
import functools

import jax
import jax.numpy as jnp
from jax import lax
from jax.experimental import pallas as pl
from jax.experimental.pallas import tpu as pltpu
from jax.sharding import PartitionSpec as P

MESH = pl.DeviceIdType.MESH
LANES = 128
TILE = 512
POOL = 4


def nt(left, right):
    return lax.dot_general(
        left, right, (((1,), (1,)), ((), ())), preferred_element_type=jnp.float32
    )


def nn(left, right):
    return lax.dot_general(
        left, right, (((1,), (0,)), ((), ())), preferred_element_type=jnp.float32
    )


def exchange(
    n_sub,
    n_grp,
    live_s,
    send_h,
    recv_h,
    counts_h,
    values_h,
    schur_h,
    basis_h,
    map_h,
    weights,
    image,
    incoming,
    high_pick,
    low_pick,
    send_s,
    recv_s,
    counts_s,
    values,
    basis,
    schur,
    cmap,
    maps,
    packed,
    arrived,
    basis_t,
    scaled_t,
    scaled,
    halves,
    part,
    pool,
    terms,
    row_pick,
    outgoing,
    load_sem,
    schur_sem,
    near_send,
    near_recv,
    pool_send,
    pool_recv,
    far_send,
    far_recv,
):
    me = lax.axis_index("sub")
    group = lax.axis_index("grp")
    n_line = n_sub // POOL
    plane, place = me // n_line, lax.rem(me, n_line)
    interface = schur.shape[0]
    columns = basis.shape[0]
    blocks = values.shape[0]
    rows = incoming.shape[1]
    section = rows * n_sub
    highs = section // LANES
    slots = packed.shape[1]

    with jax.named_scope("start_loads"):
        pairs = [
            (values_h.at[0, 0], values),
            (send_h.at[0, 0], send_s),
            (counts_h.at[0], counts_s),
            (recv_h.at[0, 0], recv_s),
            (map_h.at[0], cmap),
            (basis_h.at[0, 0], basis),
        ]
        loads = [
            pltpu.make_async_copy(source, target, load_sem.at[i])
            for i, (source, target) in enumerate(pairs)
        ]
        for load in loads[:3]:
            load.start()

    up = lax.rem(group + 1, n_grp)
    down = lax.rem(group + n_grp - 1, n_grp)
    right = lax.rem(me + 1, n_sub)
    left = lax.rem(me + n_sub - 1, n_sub)
    half = n_line // 2
    distant = [half] + [s for i in range(1, half) for s in (half - i, half + i)]
    with jax.named_scope("greet"):
        barrier = pltpu.get_barrier_semaphore()

        def greet(target):
            pl.semaphore_signal(barrier, inc=1, device_id=target, device_id_type=MESH)

        for step in distant:
            greet({"sub": plane * n_line + lax.rem(place + step, n_line)})
        for step in range(1, POOL):
            greet({"sub": lax.rem(me + step * n_line, n_sub)})
        for target in ({"sub": right}, {"sub": left}, {"grp": up}, {"grp": down}):
            greet(target)

    with jax.named_scope("start_more"):
        for load in loads[3:]:
            load.start()
        tiles = interface // TILE
        schur_loads = [
            pltpu.make_async_copy(
                schur_h.at[0, 0, pl.ds(t * TILE, TILE)],
                schur.at[pl.ds(t * TILE, TILE)],
                schur_sem.at[t],
            )
            for t in range(tiles)
        ]
        for load in schur_loads:
            load.start()

    with jax.named_scope("pack"):
        for load in loads[:3]:
            load.wait()
        for j in range(4):
            for f in range(slots):
                row = values[pl.ds(send_s[j, f], 1), :]
                packed[j, f : f + 1, :] = jnp.where(f < counts_s[0, j], row, 0.0)

    with jax.named_scope("barrier"):
        pl.semaphore_wait(barrier, 4 + (POOL - 1) + (n_line - 1))

    with jax.named_scope("near_send"):
        targets = [{"sub": right}, {"sub": left}, {"grp": up}, {"grp": down}]
        near = [
            pltpu.make_async_remote_copy(
                src_ref=packed.at[j],
                dst_ref=arrived.at[j],
                send_sem=near_send.at[j],
                recv_sem=near_recv.at[j],
                device_id=targets[j],
                device_id_type=MESH,
            )
            for j in range(4)
        ]
        for copy in near:
            copy.start()

    with jax.named_scope("picks"):
        loads[4].wait()
        wide = POOL * columns
        line_map = jnp.concatenate(
            [cmap[k * n_line : (k + 1) * n_line, :] for k in range(POOL)], axis=1
        )
        maps[...] = line_map
        mine = maps[pl.ds(place, 1), :]
        own_rows = rows * n_line
        row_at = own_rows * plane + lax.broadcasted_iota(jnp.int32, (own_rows, wide), 0)
        row_pick[...] = jnp.where(row_at == mine, 1.0, 0.0).astype(jnp.bfloat16)
        low_at = lax.broadcasted_iota(jnp.int32, (LANES, wide), 0)
        high_at = lax.broadcasted_iota(jnp.int32, (highs * rows, wide), 0) // rows

        def low(i, carry):
            row = maps[pl.ds(i, 1), :]
            at = pl.ds(pl.multiple_of(i * wide, LANES), wide)
            low_pick[:, at] = jnp.where(low_at == (row & (LANES - 1)), 1.0, 0.0).astype(
                jnp.bfloat16
            )
            return carry

        lax.fori_loop(0, n_line, low, 0)
        terms[...] = jnp.zeros_like(terms)

    with jax.named_scope("turn_basis"):
        loads[5].wait()
        for n in range(blocks):
            at = slice(n * LANES, (n + 1) * LANES)
            basis_t[at, :] = basis[:, at].astype(jnp.float32).T

    with jax.named_scope("near_wait"):
        for copy in near:
            copy.wait()
    with jax.named_scope("weights"):
        loads[3].wait()
        own = values[...]
        totals = own
        block_at = lax.broadcasted_iota(jnp.int32, own.shape, 0)
        for j in range(4):
            came = arrived[j]
            if j == 2:
                came = jnp.where(group > 0, came, 0.0)
            if j == 3:
                came = jnp.where(group < n_grp - 1, came, 0.0)
            for f in range(slots):
                totals += jnp.where(block_at == recv_s[j, f], came[f : f + 1, :], 0.0)
        weight = own / totals
        weights[0, 0] = weight

        live_size = live_s[0, 0]
        unknown = block_at * LANES + lax.broadcasted_iota(jnp.int32, own.shape, 1)
        live_weight = jnp.where(unknown < live_size, weight, 0.0)
    with jax.named_scope("scaled"):
        columns_of = live_weight.T
        for n in range(blocks):
            at = slice(n * LANES, (n + 1) * LANES)
            scaled_t[at, :] = (basis_t[at, :] * columns_of[:, n : n + 1]).astype(jnp.bfloat16)
            scaled[:, at] = (basis[:, at].astype(jnp.float32) * live_weight[n : n + 1, :]).astype(
                jnp.bfloat16
            )

    with jax.named_scope("schur_wait"):
        for load in schur_loads:
            load.wait()
    with jax.named_scope("image"):
        for t in range(tiles):
            at = slice(t * TILE, (t + 1) * TILE)
            value = nn(schur[at, :], scaled_t[...])
            row = t * TILE + lax.broadcasted_iota(jnp.int32, value.shape, 0)
            value = jnp.where(row < live_size, value, 0.0)
            top = value.astype(jnp.bfloat16)
            rest = (value - top.astype(jnp.float32)).astype(jnp.bfloat16)
            halves[at, :columns] = top
            halves[at, LANES : LANES + columns] = rest
    with jax.named_scope("part"):
        total = nn(scaled[...], halves[...])
        total = total[:, :columns] + total[:, LANES:]
        value = jnp.concatenate(
            [total / interface, jnp.zeros((columns, LANES - columns), jnp.float32)], axis=1
        )
        part[...] = pltpu.roll(value, lax.rem(columns * plane, LANES), 1).astype(jnp.bfloat16)

    with jax.named_scope("pool_send"):
        shared = []
        for step in range(1, POOL):
            other = lax.rem(plane + step, POOL)
            copy = pltpu.make_async_remote_copy(
                src_ref=part,
                dst_ref=pool.at[plane],
                send_sem=pool_send.at[step],
                recv_sem=pool_recv.at[plane],
                device_id={"sub": other * n_line + place},
                device_id_type=MESH,
            )
            copy.start()
            shared.append(copy)
    with jax.named_scope("pool_wait"):
        for step in range(1, POOL):
            other = lax.rem(plane + step, POOL)
            pltpu.make_async_copy(pool.at[other], pool.at[other], pool_recv.at[other]).wait()
        pool[pl.ds(plane, 1)] = part[...][None]
    with jax.named_scope("pick_rows"):
        lane = lax.broadcasted_iota(jnp.int32, (columns, LANES), 1)
        for k in range(POOL):
            first, last = k * columns, (k + 1) * columns
            for t in range(first // LANES, (last - 1) // LANES + 1):
                inside = (lane + t * LANES >= first) & (lane + t * LANES < last)
                keep = jnp.where(inside, 1.0, 0.0).astype(jnp.bfloat16)
                terms[first:last, t * LANES : (t + 1) * LANES] = pool[k] * keep
        picked = nn(row_pick[...], terms[...])
        outgoing[...] = picked.astype(jnp.bfloat16).reshape(outgoing.shape)

    def far(step):
        peer = lax.rem(place + step, n_line)
        return pltpu.make_async_remote_copy(
            src_ref=outgoing.at[peer],
            dst_ref=incoming.at[place],
            send_sem=far_send.at[step],
            recv_sem=far_recv.at[place],
            device_id={"sub": plane * n_line + peer},
            device_id_type=MESH,
        )

    with jax.named_scope("far_send"):
        sent = [far(step) for step in distant]
        for copy in sent:
            copy.start()

    def high(i, carry):
        row = maps[pl.ds(i, 1), :]
        at = pl.ds(pl.multiple_of(i * wide, LANES), wide)
        high_pick[:, at] = jnp.where(high_at == (row >> 7), 1.0, 0.0).astype(jnp.bfloat16)
        return carry

    with jax.named_scope("high"):
        lax.fori_loop(0, n_line, high, 0)
    with jax.named_scope("turn_image"):
        for n in range(blocks):
            at = slice(n * LANES, (n + 1) * LANES)
            image[0, 0, :, at] = halves[at, :columns].astype(jnp.float32).T.astype(jnp.bfloat16)
    with jax.named_scope("arrive"):
        for step in range(1, n_line):
            source = lax.rem(place + n_line - step, n_line)
            pltpu.make_async_copy(
                incoming.at[source], incoming.at[source], far_recv.at[source]
            ).wait()
        incoming[pl.ds(place, 1)] = outgoing[pl.ds(place, 1)]
    with jax.named_scope("drain"):
        for copy in shared + sent:
            copy.wait_send()


def assemble(
    weights,
    image,
    incoming,
    high_pick,
    low_pick,
    weights_h,
    image_h,
    coarse_h,
    spread,
    coarse,
    store_sem,
):
    rows = incoming.shape[1]
    n_line, _, wide = incoming.shape
    highs = high_pick.shape[0] // rows
    weights_out = pltpu.make_async_copy(weights, weights_h, store_sem.at[0])
    weights_out.start()
    image_out = pltpu.make_async_copy(image, image_h, store_sem.at[1])
    image_out.start()

    def fan(i, carry):
        at = pl.ds(pl.multiple_of(i * wide, LANES), wide)
        block = incoming[i]
        for h in range(highs):
            spread[h * rows : (h + 1) * rows, at] = (
                block * high_pick[h * rows : (h + 1) * rows, at]
            )
        return carry

    with jax.named_scope("fan"):
        lax.fori_loop(0, n_line, fan, 0)
    with jax.named_scope("add"):
        summed = nt(spread[...], low_pick[...])
        for h in range(highs):
            coarse[0, :, h * LANES : (h + 1) * LANES] = summed[h * rows : (h + 1) * rows, :]
    with jax.named_scope("store"):
        coarse_out = pltpu.make_async_copy(coarse, coarse_h, store_sem.at[2])
        coarse_out.start()
        weights_out.wait()
        image_out.wait()
        coarse_out.wait()


def solution(mesh):
    n_sub, n_grp = mesh.shape["sub"], mesh.shape["grp"]

    def shards(
        interface_values, send_blocks, recv_blocks, block_counts, live_sizes, schur, basis, coarse_map
    ):
        blocks, width = interface_values.shape[2:]
        slots = send_blocks.shape[3]
        interface = schur.shape[2]
        columns = basis.shape[2]
        rows = 16
        section = rows * n_sub
        highs = section // LANES
        n_line = n_sub // POOL
        wide = POOL * columns
        f32, bf16, i32 = jnp.float32, jnp.bfloat16, jnp.int32
        hbm = pl.BlockSpec(memory_space=pltpu.HBM)
        vmem = pl.BlockSpec(memory_space=pltpu.VMEM)
        pinned = [
            pltpu.with_memory_space_constraint(x, pltpu.HBM)
            for x in (send_blocks, recv_blocks, block_counts, interface_values, schur, basis, coarse_map)
        ]
        made = pl.pallas_call(
            functools.partial(exchange, n_sub, n_grp),
            out_shape=(
                jax.ShapeDtypeStruct((1, 1, blocks, width), f32),
                jax.ShapeDtypeStruct((1, 1, columns, interface), bf16),
                jax.ShapeDtypeStruct((n_line, rows, wide), bf16),
                jax.ShapeDtypeStruct((highs * rows, n_line * wide), bf16),
                jax.ShapeDtypeStruct((LANES, n_line * wide), bf16),
            ),
            in_specs=[pl.BlockSpec(memory_space=pltpu.SMEM)] + [hbm] * 7,
            out_specs=(vmem,) * 5,
            scratch_shapes=[
                pltpu.SMEM((4, slots), i32),
                pltpu.SMEM((4, slots), i32),
                pltpu.SMEM((1, 4), i32),
                pltpu.VMEM((blocks, width), f32),
                pltpu.VMEM((columns, interface), bf16),
                pltpu.VMEM((interface, interface), bf16),
                pltpu.VMEM((n_sub, columns), i32),
                pltpu.VMEM((n_line, wide), i32),
                pltpu.VMEM((4, slots, width), f32),
                pltpu.VMEM((4, slots, width), f32),
                pltpu.VMEM((interface, columns), f32),
                pltpu.VMEM((interface, columns), bf16),
                pltpu.VMEM((columns, interface), bf16),
                pltpu.VMEM((interface, LANES + columns), bf16),
                pltpu.VMEM((columns, LANES), bf16),
                pltpu.VMEM((POOL, columns, LANES), bf16),
                pltpu.VMEM((wide, wide), bf16),
                pltpu.VMEM((rows * n_line, wide), bf16),
                pltpu.VMEM((n_line, rows, wide), bf16),
                pltpu.SemaphoreType.DMA((6,)),
                pltpu.SemaphoreType.DMA((interface // TILE,)),
                pltpu.SemaphoreType.DMA((4,)),
                pltpu.SemaphoreType.DMA((4,)),
                pltpu.SemaphoreType.DMA((POOL,)),
                pltpu.SemaphoreType.DMA((POOL,)),
                pltpu.SemaphoreType.DMA((n_line,)),
                pltpu.SemaphoreType.DMA((n_line,)),
            ],
            compiler_params=pltpu.CompilerParams(
                collective_id=0, has_side_effects=True, vmem_limit_bytes=32 * 1024 * 1024
            ),
        )(live_sizes, *pinned)
        return pl.pallas_call(
            assemble,
            out_shape=(
                jax.ShapeDtypeStruct((1, 1, blocks, width), f32),
                jax.ShapeDtypeStruct((1, 1, columns, interface), bf16),
                jax.ShapeDtypeStruct((1, rows, section), f32),
            ),
            in_specs=[vmem] * 5,
            out_specs=(hbm,) * 3,
            scratch_shapes=[
                pltpu.VMEM((highs * rows, n_line * wide), bf16),
                pltpu.VMEM((1, rows, section), f32),
                pltpu.SemaphoreType.DMA((3,)),
            ],
            compiler_params=pltpu.CompilerParams(vmem_limit_bytes=16 * 1024 * 1024),
        )(*made)

    placed = (
        P("grp", "sub", None, None),
        P("grp", "sub", None, None),
        P("grp", "sub", None, None),
        P("grp", "sub", None),
        P("grp", "sub"),
        P("grp", "sub", None, None),
        P("grp", "sub", None, None),
        P("grp", None, None),
    )
    return jax.shard_map(
        shards,
        mesh=mesh,
        in_specs=placed,
        out_specs=(P("grp", "sub", None, None), P("grp", "sub", None, None), P("grp", "sub", None)),
        check_vma=False,
    )
```

```python
import functools

import jax
import jax.numpy as jnp
from jax import lax
from jax.experimental import pallas as pl
from jax.experimental.pallas import tpu as pltpu
from jax.sharding import PartitionSpec as P

MESH = pl.DeviceIdType.MESH
LANES = 128
TILE = 512
POOL = 4


def nt(left, right):
    return lax.dot_general(
        left, right, (((1,), (1,)), ((), ())), preferred_element_type=jnp.float32
    )


def nn(left, right):
    return lax.dot_general(
        left, right, (((1,), (0,)), ((), ())), preferred_element_type=jnp.float32
    )


def exchange(
    n_sub,
    n_grp,
    live_s,
    send_h,
    recv_h,
    counts_h,
    values_h,
    schur_h,
    basis_h,
    map_h,
    weights,
    image,
    incoming,
    high_pick,
    low_pick,
    send_s,
    recv_s,
    counts_s,
    values,
    basis,
    schur,
    cmap,
    maps,
    packed,
    arrived,
    basis_t,
    scaled_t,
    scaled,
    halves,
    part,
    pool,
    terms,
    row_pick,
    outgoing,
    load_sem,
    schur_sem,
    near_send,
    near_recv,
    pool_send,
    pool_recv,
    far_send,
    far_recv,
):
    me = lax.axis_index("sub")
    group = lax.axis_index("grp")
    n_line = n_sub // POOL
    plane, place = me // n_line, lax.rem(me, n_line)
    interface = schur.shape[0]
    columns = basis.shape[0]
    blocks = values.shape[0]
    rows = incoming.shape[1]
    section = rows * n_sub
    highs = section // LANES
    slots = packed.shape[1]

    with jax.named_scope("start_loads"):
        pairs = [
            (values_h.at[0, 0], values),
            (send_h.at[0, 0], send_s),
            (counts_h.at[0], counts_s),
            (recv_h.at[0, 0], recv_s),
            (map_h.at[0], cmap),
            (basis_h.at[0, 0], basis),
        ]
        loads = [
            pltpu.make_async_copy(source, target, load_sem.at[i])
            for i, (source, target) in enumerate(pairs)
        ]
        for load in loads[:3]:
            load.start()

    up = lax.rem(group + 1, n_grp)
    down = lax.rem(group + n_grp - 1, n_grp)
    right = lax.rem(me + 1, n_sub)
    left = lax.rem(me + n_sub - 1, n_sub)
    apart = [min(step, n_line - step) for step in range(n_line)]
    distant = sorted(
        range(1, n_line), key=lambda step: (-((apart[step] + 1) // 2), -(apart[step] % 2))
    )
    with jax.named_scope("greet"):
        barrier = pltpu.get_barrier_semaphore()

        def greet(target):
            pl.semaphore_signal(barrier, inc=1, device_id=target, device_id_type=MESH)

        for step in distant:
            greet({"sub": plane * n_line + lax.rem(place + step, n_line)})
        for step in range(1, POOL):
            greet({"sub": lax.rem(me + step * n_line, n_sub)})
        for target in ({"sub": right}, {"sub": left}, {"grp": up}, {"grp": down}):
            greet(target)

    with jax.named_scope("start_more"):
        for load in loads[3:]:
            load.start()
        tiles = interface // TILE
        schur_loads = [
            pltpu.make_async_copy(
                schur_h.at[0, 0, pl.ds(t * TILE, TILE)],
                schur.at[pl.ds(t * TILE, TILE)],
                schur_sem.at[t],
            )
            for t in range(tiles)
        ]
        for load in schur_loads:
            load.start()

    with jax.named_scope("pack"):
        for load in loads[:3]:
            load.wait()
        for j in range(4):
            for f in range(slots):
                row = values[pl.ds(send_s[j, f], 1), :]
                packed[j, f : f + 1, :] = jnp.where(f < counts_s[0, j], row, 0.0)

    with jax.named_scope("barrier"):
        pl.semaphore_wait(barrier, 4 + (POOL - 1) + (n_line - 1))

    with jax.named_scope("near_send"):
        targets = [{"sub": right}, {"sub": left}, {"grp": up}, {"grp": down}]
        near = [
            pltpu.make_async_remote_copy(
                src_ref=packed.at[j],
                dst_ref=arrived.at[j],
                send_sem=near_send.at[j],
                recv_sem=near_recv.at[j],
                device_id=targets[j],
                device_id_type=MESH,
            )
            for j in range(4)
        ]
        for copy in near:
            copy.start()

    with jax.named_scope("picks"):
        loads[4].wait()
        wide = POOL * columns
        line_map = jnp.concatenate(
            [cmap[k * n_line : (k + 1) * n_line, :] for k in range(POOL)], axis=1
        )
        maps[...] = line_map
        mine = maps[pl.ds(place, 1), :]
        own_rows = rows * n_line
        row_at = own_rows * plane + lax.broadcasted_iota(jnp.int32, (own_rows, wide), 0)
        row_pick[...] = jnp.where(row_at == mine, 1.0, 0.0).astype(jnp.bfloat16)
        low_at = lax.broadcasted_iota(jnp.int32, (LANES, wide), 0)
        high_at = lax.broadcasted_iota(jnp.int32, (highs * rows, wide), 0) // rows

        def low(i, carry):
            row = maps[pl.ds(i, 1), :]
            at = pl.ds(pl.multiple_of(i * wide, LANES), wide)
            low_pick[:, at] = jnp.where(low_at == (row & (LANES - 1)), 1.0, 0.0).astype(
                jnp.bfloat16
            )
            return carry

        lax.fori_loop(0, n_line, low, 0)
        terms[...] = jnp.zeros_like(terms)

    with jax.named_scope("turn_basis"):
        loads[5].wait()
        for n in range(blocks):
            at = slice(n * LANES, (n + 1) * LANES)
            basis_t[at, :] = basis[:, at].astype(jnp.float32).T

    with jax.named_scope("near_wait"):
        for copy in near:
            copy.wait()
    with jax.named_scope("weights"):
        loads[3].wait()
        own = values[...]
        totals = own
        block_at = lax.broadcasted_iota(jnp.int32, own.shape, 0)
        for j in range(4):
            came = arrived[j]
            if j == 2:
                came = jnp.where(group > 0, came, 0.0)
            if j == 3:
                came = jnp.where(group < n_grp - 1, came, 0.0)
            for f in range(slots):
                totals += jnp.where(block_at == recv_s[j, f], came[f : f + 1, :], 0.0)
        weight = own / totals
        weights[0, 0] = weight

        live_size = live_s[0, 0]
        unknown = block_at * LANES + lax.broadcasted_iota(jnp.int32, own.shape, 1)
        live_weight = jnp.where(unknown < live_size, weight, 0.0)
    with jax.named_scope("scaled"):
        columns_of = live_weight.T
        for n in range(blocks):
            at = slice(n * LANES, (n + 1) * LANES)
            scaled_t[at, :] = (basis_t[at, :] * columns_of[:, n : n + 1]).astype(jnp.bfloat16)

    with jax.named_scope("schur_wait"):
        for load in schur_loads:
            load.wait()
    with jax.named_scope("image"):
        for t in range(tiles):
            for n in range(t * TILE // LANES, (t + 1) * TILE // LANES):
                at = slice(n * LANES, (n + 1) * LANES)
                scaled[:, at] = (
                    basis[:, at].astype(jnp.float32) * live_weight[n : n + 1, :]
                ).astype(jnp.bfloat16)
            at = slice(t * TILE, (t + 1) * TILE)
            value = nn(schur[at, :], scaled_t[...])
            row = t * TILE + lax.broadcasted_iota(jnp.int32, value.shape, 0)
            value = jnp.where(row < live_size, value, 0.0)
            top = value.astype(jnp.bfloat16)
            rest = (value - top.astype(jnp.float32)).astype(jnp.bfloat16)
            halves[at, :columns] = top
            halves[at, LANES : LANES + columns] = rest
    with jax.named_scope("part"):
        total = nn(scaled[...], halves[...])
        total = total[:, :columns] + total[:, LANES:]
        value = jnp.concatenate(
            [total / interface, jnp.zeros((columns, LANES - columns), jnp.float32)], axis=1
        )
        part[...] = pltpu.roll(value, lax.rem(columns * plane, LANES), 1).astype(jnp.bfloat16)

    with jax.named_scope("pool_send"):
        shared = []
        for step in sorted(range(1, POOL), key=lambda step: -min(step, POOL - step)):
            other = lax.rem(plane + step, POOL)
            copy = pltpu.make_async_remote_copy(
                src_ref=part,
                dst_ref=pool.at[plane],
                send_sem=pool_send.at[step],
                recv_sem=pool_recv.at[plane],
                device_id={"sub": other * n_line + place},
                device_id_type=MESH,
            )
            copy.start()
            shared.append(copy)
    with jax.named_scope("pool_wait"):
        for step in range(1, POOL):
            other = lax.rem(plane + step, POOL)
            pltpu.make_async_copy(pool.at[other], pool.at[other], pool_recv.at[other]).wait()
        pool[pl.ds(plane, 1)] = part[...][None]
    with jax.named_scope("pick_rows"):
        lane = lax.broadcasted_iota(jnp.int32, (columns, LANES), 1)
        for k in range(POOL):
            first, last = k * columns, (k + 1) * columns
            for t in range(first // LANES, (last - 1) // LANES + 1):
                inside = (lane + t * LANES >= first) & (lane + t * LANES < last)
                keep = jnp.where(inside, 1.0, 0.0).astype(jnp.bfloat16)
                terms[first:last, t * LANES : (t + 1) * LANES] = pool[k] * keep
        picked = nn(row_pick[...], terms[...])
        outgoing[...] = picked.astype(jnp.bfloat16).reshape(outgoing.shape)

    def far(step):
        peer = lax.rem(place + step, n_line)
        return pltpu.make_async_remote_copy(
            src_ref=outgoing.at[peer],
            dst_ref=incoming.at[place],
            send_sem=far_send.at[step],
            recv_sem=far_recv.at[place],
            device_id={"sub": plane * n_line + peer},
            device_id_type=MESH,
        )

    with jax.named_scope("far_send"):
        sent = [far(step) for step in distant]
        for copy in sent:
            copy.start()

    def high(i, carry):
        row = maps[pl.ds(i, 1), :]
        at = pl.ds(pl.multiple_of(i * wide, LANES), wide)
        high_pick[:, at] = jnp.where(high_at == (row >> 7), 1.0, 0.0).astype(jnp.bfloat16)
        return carry

    with jax.named_scope("high"):
        lax.fori_loop(0, n_line, high, 0)
    with jax.named_scope("turn_image"):
        for n in range(blocks):
            at = slice(n * LANES, (n + 1) * LANES)
            image[0, 0, :, at] = halves[at, :columns].astype(jnp.float32).T.astype(jnp.bfloat16)
    with jax.named_scope("arrive"):
        for step in range(1, n_line):
            source = lax.rem(place + n_line - step, n_line)
            pltpu.make_async_copy(
                incoming.at[source], incoming.at[source], far_recv.at[source]
            ).wait()
        incoming[pl.ds(place, 1)] = outgoing[pl.ds(place, 1)]
    with jax.named_scope("drain"):
        for copy in shared + sent:
            copy.wait_send()


def assemble(
    weights,
    image,
    incoming,
    high_pick,
    low_pick,
    weights_h,
    image_h,
    coarse_h,
    spread,
    coarse,
    store_sem,
):
    rows = incoming.shape[1]
    n_line, _, wide = incoming.shape
    highs = high_pick.shape[0] // rows
    weights_out = pltpu.make_async_copy(weights, weights_h, store_sem.at[0])
    weights_out.start()
    image_out = pltpu.make_async_copy(image, image_h, store_sem.at[1])
    image_out.start()

    def fan(i, carry):
        at = slice(i * wide, (i + 1) * wide)
        block = incoming[i]
        for h in range(highs):
            spread[h * rows : (h + 1) * rows, at] = (
                block * high_pick[h * rows : (h + 1) * rows, at]
            )
        return carry

    with jax.named_scope("fan"):
        for i in range(n_line):
            fan(i, 0)
    with jax.named_scope("add"):
        summed = nt(spread[...], low_pick[...])
        for h in range(highs):
            coarse[0, :, h * LANES : (h + 1) * LANES] = summed[h * rows : (h + 1) * rows, :]
    with jax.named_scope("store"):
        coarse_out = pltpu.make_async_copy(coarse, coarse_h, store_sem.at[2])
        coarse_out.start()
        weights_out.wait()
        image_out.wait()
        coarse_out.wait()


def solution(mesh):
    n_sub, n_grp = mesh.shape["sub"], mesh.shape["grp"]

    def shards(
        interface_values, send_blocks, recv_blocks, block_counts, live_sizes, schur, basis, coarse_map
    ):
        blocks, width = interface_values.shape[2:]
        slots = send_blocks.shape[3]
        interface = schur.shape[2]
        columns = basis.shape[2]
        rows = 16
        section = rows * n_sub
        highs = section // LANES
        n_line = n_sub // POOL
        wide = POOL * columns
        f32, bf16, i32 = jnp.float32, jnp.bfloat16, jnp.int32
        hbm = pl.BlockSpec(memory_space=pltpu.HBM)
        vmem = pl.BlockSpec(memory_space=pltpu.VMEM)
        pinned = [
            pltpu.with_memory_space_constraint(x, pltpu.HBM)
            for x in (send_blocks, recv_blocks, block_counts, interface_values, schur, basis, coarse_map)
        ]
        made = pl.pallas_call(
            functools.partial(exchange, n_sub, n_grp),
            out_shape=(
                jax.ShapeDtypeStruct((1, 1, blocks, width), f32),
                jax.ShapeDtypeStruct((1, 1, columns, interface), bf16),
                jax.ShapeDtypeStruct((n_line, rows, wide), bf16),
                jax.ShapeDtypeStruct((highs * rows, n_line * wide), bf16),
                jax.ShapeDtypeStruct((LANES, n_line * wide), bf16),
            ),
            in_specs=[pl.BlockSpec(memory_space=pltpu.SMEM)] + [hbm] * 7,
            out_specs=(vmem,) * 5,
            scratch_shapes=[
                pltpu.SMEM((4, slots), i32),
                pltpu.SMEM((4, slots), i32),
                pltpu.SMEM((1, 4), i32),
                pltpu.VMEM((blocks, width), f32),
                pltpu.VMEM((columns, interface), bf16),
                pltpu.VMEM((interface, interface), bf16),
                pltpu.VMEM((n_sub, columns), i32),
                pltpu.VMEM((n_line, wide), i32),
                pltpu.VMEM((4, slots, width), f32),
                pltpu.VMEM((4, slots, width), f32),
                pltpu.VMEM((interface, columns), f32),
                pltpu.VMEM((interface, columns), bf16),
                pltpu.VMEM((columns, interface), bf16),
                pltpu.VMEM((interface, LANES + columns), bf16),
                pltpu.VMEM((columns, LANES), bf16),
                pltpu.VMEM((POOL, columns, LANES), bf16),
                pltpu.VMEM((wide, wide), bf16),
                pltpu.VMEM((rows * n_line, wide), bf16),
                pltpu.VMEM((n_line, rows, wide), bf16),
                pltpu.SemaphoreType.DMA((6,)),
                pltpu.SemaphoreType.DMA((interface // TILE,)),
                pltpu.SemaphoreType.DMA((4,)),
                pltpu.SemaphoreType.DMA((4,)),
                pltpu.SemaphoreType.DMA((POOL,)),
                pltpu.SemaphoreType.DMA((POOL,)),
                pltpu.SemaphoreType.DMA((n_line,)),
                pltpu.SemaphoreType.DMA((n_line,)),
            ],
            compiler_params=pltpu.CompilerParams(
                collective_id=0, has_side_effects=True, vmem_limit_bytes=32 * 1024 * 1024
            ),
        )(live_sizes, *pinned)
        return pl.pallas_call(
            assemble,
            out_shape=(
                jax.ShapeDtypeStruct((1, 1, blocks, width), f32),
                jax.ShapeDtypeStruct((1, 1, columns, interface), bf16),
                jax.ShapeDtypeStruct((1, rows, section), f32),
            ),
            in_specs=[vmem] * 5,
            out_specs=(hbm,) * 3,
            scratch_shapes=[
                pltpu.VMEM((highs * rows, n_line * wide), bf16),
                pltpu.VMEM((1, rows, section), f32),
                pltpu.SemaphoreType.DMA((3,)),
            ],
            compiler_params=pltpu.CompilerParams(vmem_limit_bytes=16 * 1024 * 1024),
        )(*made)

    placed = (
        P("grp", "sub", None, None),
        P("grp", "sub", None, None),
        P("grp", "sub", None, None),
        P("grp", "sub", None),
        P("grp", "sub"),
        P("grp", "sub", None, None),
        P("grp", "sub", None, None),
        P("grp", None, None),
    )
    return jax.shard_map(
        shards,
        mesh=mesh,
        in_specs=placed,
        out_specs=(P("grp", "sub", None, None), P("grp", "sub", None, None), P("grp", "sub", None)),
        check_vma=False,
    )
```

```python
import functools

import jax
import jax.numpy as jnp
from jax import lax
from jax.experimental import pallas as pl
from jax.experimental.pallas import tpu as pltpu
from jax.sharding import PartitionSpec as P

MESH = pl.DeviceIdType.MESH
LANES = 128
TILE = 512
POOL = 4


def nt(left, right):
    return lax.dot_general(
        left, right, (((1,), (1,)), ((), ())), preferred_element_type=jnp.float32
    )


def nn(left, right):
    return lax.dot_general(
        left, right, (((1,), (0,)), ((), ())), preferred_element_type=jnp.float32
    )


def exchange(
    n_sub,
    n_grp,
    live_s,
    send_h,
    recv_h,
    counts_h,
    values_h,
    schur_h,
    basis_h,
    map_h,
    weights,
    image,
    incoming,
    high_pick,
    low_pick,
    send_s,
    recv_s,
    counts_s,
    values,
    basis,
    schur,
    cmap,
    maps,
    packed,
    arrived,
    basis_t,
    scaled_t,
    scaled,
    halves,
    part,
    pool,
    terms,
    row_pick,
    outgoing,
    load_sem,
    schur_sem,
    near_send,
    near_recv,
    pool_send,
    pool_recv,
    far_send,
    far_recv,
):
    me = lax.axis_index("sub")
    group = lax.axis_index("grp")
    n_line = n_sub // POOL
    plane, place = me // n_line, lax.rem(me, n_line)
    interface = schur.shape[0]
    columns = basis.shape[0]
    blocks = values.shape[0]
    rows = incoming.shape[1]
    section = rows * n_sub
    highs = section // LANES
    slots = packed.shape[1]

    with jax.named_scope("start_loads"):
        pairs = [
            (values_h.at[0, 0], values),
            (send_h.at[0, 0], send_s),
            (counts_h.at[0], counts_s),
            (recv_h.at[0, 0], recv_s),
            (map_h.at[0], cmap),
            (basis_h.at[0, 0], basis),
        ]
        loads = [
            pltpu.make_async_copy(source, target, load_sem.at[i])
            for i, (source, target) in enumerate(pairs)
        ]
        for load in loads[:3]:
            load.start()

    up = lax.rem(group + 1, n_grp)
    down = lax.rem(group + n_grp - 1, n_grp)
    right = lax.rem(me + 1, n_sub)
    left = lax.rem(me + n_sub - 1, n_sub)
    apart = [min(step, n_line - step) for step in range(n_line)]
    distant = sorted(
        range(1, n_line), key=lambda step: (-((apart[step] + 1) // 2), -(apart[step] % 2))
    )
    with jax.named_scope("greet"):
        barrier = pltpu.get_barrier_semaphore()

        def greet(target):
            pl.semaphore_signal(barrier, inc=1, device_id=target, device_id_type=MESH)

        for step in distant:
            greet({"sub": plane * n_line + lax.rem(place + step, n_line)})
        for step in range(1, POOL):
            greet({"sub": lax.rem(me + step * n_line, n_sub)})
        for target in ({"sub": right}, {"sub": left}, {"grp": up}, {"grp": down}):
            greet(target)

    with jax.named_scope("start_more"):
        for load in loads[3:]:
            load.start()
        tiles = interface // TILE
        schur_loads = [
            pltpu.make_async_copy(
                schur_h.at[0, 0, pl.ds(t * TILE, TILE)],
                schur.at[pl.ds(t * TILE, TILE)],
                schur_sem.at[t],
            )
            for t in range(tiles)
        ]
        for load in schur_loads:
            load.start()

    with jax.named_scope("pack"):
        for load in loads[:3]:
            load.wait()
        for j in range(4):
            for f in range(slots):
                row = values[pl.ds(send_s[j, f], 1), :]
                packed[j, f : f + 1, :] = jnp.where(f < counts_s[0, j], row, 0.0)

    with jax.named_scope("barrier"):
        pl.semaphore_wait(barrier, 4 + (POOL - 1) + (n_line - 1))

    with jax.named_scope("near_send"):
        targets = [{"sub": right}, {"sub": left}, {"grp": up}, {"grp": down}]
        near = [
            pltpu.make_async_remote_copy(
                src_ref=packed.at[j],
                dst_ref=arrived.at[j],
                send_sem=near_send.at[j],
                recv_sem=near_recv.at[j],
                device_id=targets[j],
                device_id_type=MESH,
            )
            for j in range(4)
        ]
        for copy in near:
            copy.start()

    with jax.named_scope("picks"):
        loads[4].wait()
        wide = POOL * columns
        line_map = jnp.concatenate(
            [cmap[k * n_line : (k + 1) * n_line, :] for k in range(POOL)], axis=1
        )
        maps[...] = line_map
        mine = maps[pl.ds(place, 1), :]
        row_at = lax.broadcasted_iota(jnp.int32, (rows, wide), 0)
        for i, step in enumerate(distant + [0]):
            owner = plane * n_line + lax.rem(place + step, n_line)
            row_pick[i * rows : (i + 1) * rows, :] = jnp.where(
                row_at == mine - rows * owner, 1.0, 0.0
            ).astype(jnp.bfloat16)
        low_at = lax.broadcasted_iota(jnp.int32, (LANES, wide), 0)
        high_at = lax.broadcasted_iota(jnp.int32, (highs * rows, wide), 0) // rows

        def low(i, carry):
            row = maps[pl.ds(i, 1), :]
            at = pl.ds(pl.multiple_of(i * wide, LANES), wide)
            low_pick[:, at] = jnp.where(low_at == (row & (LANES - 1)), 1.0, 0.0).astype(
                jnp.bfloat16
            )
            return carry

        lax.fori_loop(0, n_line, low, 0)
        terms[...] = jnp.zeros_like(terms)

    with jax.named_scope("turn_basis"):
        loads[5].wait()
        for n in range(blocks):
            at = slice(n * LANES, (n + 1) * LANES)
            basis_t[at, :] = basis[:, at].astype(jnp.float32).T

    with jax.named_scope("near_wait"):
        for copy in near:
            copy.wait()
    with jax.named_scope("weights"):
        loads[3].wait()
        own = values[...]
        totals = own
        block_at = lax.broadcasted_iota(jnp.int32, own.shape, 0)
        for j in range(4):
            came = arrived[j]
            if j == 2:
                came = jnp.where(group > 0, came, 0.0)
            if j == 3:
                came = jnp.where(group < n_grp - 1, came, 0.0)
            for f in range(slots):
                totals += jnp.where(block_at == recv_s[j, f], came[f : f + 1, :], 0.0)
        weight = own / totals
        weights[0, 0] = weight

        live_size = live_s[0, 0]
        unknown = block_at * LANES + lax.broadcasted_iota(jnp.int32, own.shape, 1)
        live_weight = jnp.where(unknown < live_size, weight, 0.0)
    with jax.named_scope("scaled"):
        columns_of = live_weight.T
        for n in range(blocks):
            at = slice(n * LANES, (n + 1) * LANES)
            scaled_t[at, :] = (basis_t[at, :] * columns_of[:, n : n + 1]).astype(jnp.bfloat16)

    with jax.named_scope("schur_wait"):
        for load in schur_loads:
            load.wait()
    with jax.named_scope("image"):
        for t in range(tiles):
            for n in range(t * TILE // LANES, (t + 1) * TILE // LANES):
                at = slice(n * LANES, (n + 1) * LANES)
                scaled[:, at] = (
                    basis[:, at].astype(jnp.float32) * live_weight[n : n + 1, :]
                ).astype(jnp.bfloat16)
            at = slice(t * TILE, (t + 1) * TILE)
            value = nn(schur[at, :], scaled_t[...])
            row = t * TILE + lax.broadcasted_iota(jnp.int32, value.shape, 0)
            value = jnp.where(row < live_size, value, 0.0)
            top = value.astype(jnp.bfloat16)
            rest = (value - top.astype(jnp.float32)).astype(jnp.bfloat16)
            halves[at, :columns] = top
            halves[at, LANES : LANES + columns] = rest
    with jax.named_scope("part"):
        total = nn(scaled[...], halves[...])
        total = total[:, :columns] + total[:, LANES:]
        value = jnp.concatenate(
            [total * (1.0 / interface), jnp.zeros((columns, LANES - columns), jnp.float32)], axis=1
        )
        part[...] = pltpu.roll(value, lax.rem(columns * plane, LANES), 1).astype(jnp.bfloat16)

    with jax.named_scope("pool_send"):
        shared = []
        for step in sorted(range(1, POOL), key=lambda step: -min(step, POOL - step)):
            other = lax.rem(plane + step, POOL)
            copy = pltpu.make_async_remote_copy(
                src_ref=part,
                dst_ref=pool.at[plane],
                send_sem=pool_send.at[step],
                recv_sem=pool_recv.at[plane],
                device_id={"sub": other * n_line + place},
                device_id_type=MESH,
            )
            copy.start()
            shared.append(copy)
    with jax.named_scope("pool_wait"):
        for step in range(1, POOL):
            other = lax.rem(plane + step, POOL)
            pltpu.make_async_copy(pool.at[other], pool.at[other], pool_recv.at[other]).wait()
        pool[pl.ds(plane, 1)] = part[...][None]
    with jax.named_scope("pick_rows"):
        lane = lax.broadcasted_iota(jnp.int32, (columns, LANES), 1)
        for k in range(POOL):
            first, last = k * columns, (k + 1) * columns
            for t in range(first // LANES, (last - 1) // LANES + 1):
                inside = (lane + t * LANES >= first) & (lane + t * LANES < last)
                keep = jnp.where(inside, 1.0, 0.0).astype(jnp.bfloat16)
                terms[first:last, t * LANES : (t + 1) * LANES] = pool[k] * keep

    def far(i, step):
        peer = lax.rem(place + step, n_line)
        return pltpu.make_async_remote_copy(
            src_ref=outgoing.at[i],
            dst_ref=incoming.at[place],
            send_sem=far_send.at[i],
            recv_sem=far_recv.at[place],
            device_id={"sub": plane * n_line + peer},
            device_id_type=MESH,
        )

    sent = []
    half = n_line // 2
    for first in (0, half):
        with jax.named_scope("pick_rows"):
            picked = nn(row_pick[first * rows : (first + half) * rows, :], terms[...])
            outgoing[first : first + half] = picked.astype(jnp.bfloat16).reshape(half, rows, wide)
        with jax.named_scope("far_send"):
            for i in range(first, min(first + half, n_line - 1)):
                sent.append(far(i, distant[i]))
                sent[-1].start()

    def high(i, carry):
        row = maps[pl.ds(i, 1), :]
        at = pl.ds(pl.multiple_of(i * wide, LANES), wide)
        high_pick[:, at] = jnp.where(high_at == (row >> 7), 1.0, 0.0).astype(jnp.bfloat16)
        return carry

    with jax.named_scope("high"):
        lax.fori_loop(0, n_line, high, 0)
    with jax.named_scope("turn_image"):
        for n in range(blocks):
            at = slice(n * LANES, (n + 1) * LANES)
            image[0, 0, :, at] = halves[at, :columns].astype(jnp.float32).T.astype(jnp.bfloat16)
    with jax.named_scope("arrive"):
        for step in range(1, n_line):
            source = lax.rem(place + n_line - step, n_line)
            pltpu.make_async_copy(
                incoming.at[source], incoming.at[source], far_recv.at[source]
            ).wait()
        incoming[pl.ds(place, 1)] = outgoing[n_line - 1 : n_line]
    with jax.named_scope("drain"):
        for copy in shared + sent:
            copy.wait_send()


def assemble(
    weights,
    image,
    incoming,
    high_pick,
    low_pick,
    weights_h,
    image_h,
    coarse_h,
    spread,
    coarse,
    store_sem,
):
    rows = incoming.shape[1]
    n_line, _, wide = incoming.shape
    highs = high_pick.shape[0] // rows
    weights_out = pltpu.make_async_copy(weights, weights_h, store_sem.at[0])
    weights_out.start()
    image_out = pltpu.make_async_copy(image, image_h, store_sem.at[1])
    image_out.start()

    def fan(i, carry):
        at = slice(i * wide, (i + 1) * wide)
        block = incoming[i]
        for h in range(highs):
            spread[h * rows : (h + 1) * rows, at] = (
                block * high_pick[h * rows : (h + 1) * rows, at]
            )
        return carry

    with jax.named_scope("fan"):
        for i in range(n_line):
            fan(i, 0)
    with jax.named_scope("add"):
        summed = nt(spread[...], low_pick[...])
        for h in range(highs):
            coarse[0, :, h * LANES : (h + 1) * LANES] = summed[h * rows : (h + 1) * rows, :]
    with jax.named_scope("store"):
        coarse_out = pltpu.make_async_copy(coarse, coarse_h, store_sem.at[2])
        coarse_out.start()
        weights_out.wait()
        image_out.wait()
        coarse_out.wait()


def solution(mesh):
    n_sub, n_grp = mesh.shape["sub"], mesh.shape["grp"]

    def shards(
        interface_values, send_blocks, recv_blocks, block_counts, live_sizes, schur, basis, coarse_map
    ):
        blocks, width = interface_values.shape[2:]
        slots = send_blocks.shape[3]
        interface = schur.shape[2]
        columns = basis.shape[2]
        rows = 16
        section = rows * n_sub
        highs = section // LANES
        n_line = n_sub // POOL
        wide = POOL * columns
        f32, bf16, i32 = jnp.float32, jnp.bfloat16, jnp.int32
        hbm = pl.BlockSpec(memory_space=pltpu.HBM)
        vmem = pl.BlockSpec(memory_space=pltpu.VMEM)
        pinned = [
            pltpu.with_memory_space_constraint(x, pltpu.HBM)
            for x in (send_blocks, recv_blocks, block_counts, interface_values, schur, basis, coarse_map)
        ]
        made = pl.pallas_call(
            functools.partial(exchange, n_sub, n_grp),
            out_shape=(
                jax.ShapeDtypeStruct((1, 1, blocks, width), f32),
                jax.ShapeDtypeStruct((1, 1, columns, interface), bf16),
                jax.ShapeDtypeStruct((n_line, rows, wide), bf16),
                jax.ShapeDtypeStruct((highs * rows, n_line * wide), bf16),
                jax.ShapeDtypeStruct((LANES, n_line * wide), bf16),
            ),
            in_specs=[pl.BlockSpec(memory_space=pltpu.SMEM)] + [hbm] * 7,
            out_specs=(vmem,) * 5,
            scratch_shapes=[
                pltpu.SMEM((4, slots), i32),
                pltpu.SMEM((4, slots), i32),
                pltpu.SMEM((1, 4), i32),
                pltpu.VMEM((blocks, width), f32),
                pltpu.VMEM((columns, interface), bf16),
                pltpu.VMEM((interface, interface), bf16),
                pltpu.VMEM((n_sub, columns), i32),
                pltpu.VMEM((n_line, wide), i32),
                pltpu.VMEM((4, slots, width), f32),
                pltpu.VMEM((4, slots, width), f32),
                pltpu.VMEM((interface, columns), f32),
                pltpu.VMEM((interface, columns), bf16),
                pltpu.VMEM((columns, interface), bf16),
                pltpu.VMEM((interface, LANES + columns), bf16),
                pltpu.VMEM((columns, LANES), bf16),
                pltpu.VMEM((POOL, columns, LANES), bf16),
                pltpu.VMEM((wide, wide), bf16),
                pltpu.VMEM((rows * n_line, wide), bf16),
                pltpu.VMEM((n_line, rows, wide), bf16),
                pltpu.SemaphoreType.DMA((6,)),
                pltpu.SemaphoreType.DMA((interface // TILE,)),
                pltpu.SemaphoreType.DMA((4,)),
                pltpu.SemaphoreType.DMA((4,)),
                pltpu.SemaphoreType.DMA((POOL,)),
                pltpu.SemaphoreType.DMA((POOL,)),
                pltpu.SemaphoreType.DMA((n_line,)),
                pltpu.SemaphoreType.DMA((n_line,)),
            ],
            compiler_params=pltpu.CompilerParams(
                collective_id=0, has_side_effects=True, vmem_limit_bytes=32 * 1024 * 1024
            ),
        )(live_sizes, *pinned)
        return pl.pallas_call(
            assemble,
            out_shape=(
                jax.ShapeDtypeStruct((1, 1, blocks, width), f32),
                jax.ShapeDtypeStruct((1, 1, columns, interface), bf16),
                jax.ShapeDtypeStruct((1, rows, section), f32),
            ),
            in_specs=[vmem] * 5,
            out_specs=(hbm,) * 3,
            scratch_shapes=[
                pltpu.VMEM((highs * rows, n_line * wide), bf16),
                pltpu.VMEM((1, rows, section), f32),
                pltpu.SemaphoreType.DMA((3,)),
            ],
            compiler_params=pltpu.CompilerParams(vmem_limit_bytes=16 * 1024 * 1024),
        )(*made)

    placed = (
        P("grp", "sub", None, None),
        P("grp", "sub", None, None),
        P("grp", "sub", None, None),
        P("grp", "sub", None),
        P("grp", "sub"),
        P("grp", "sub", None, None),
        P("grp", "sub", None, None),
        P("grp", None, None),
    )
    return jax.shard_map(
        shards,
        mesh=mesh,
        in_specs=placed,
        out_specs=(P("grp", "sub", None, None), P("grp", "sub", None, None), P("grp", "sub", None)),
        check_vma=False,
    )
```
